32 devices in a mesh: section: 4 (over x, core), rows: 8 (over z, y).
Axes of the slice: x: 2, y: 2, z: 4, core: 2. Of those that a mesh axis runs over, the one named last changes fastest.
Arguments:
- fwd_in: bfloat16 [4, 128, 32, 512], P('section', 'rows'), may hold values from -6 to 6
- grad_in: bfloat16 [4, 128, 32, 512], P('section', 'rows'), may hold values from -6 to 6
- saved_in: bfloat16 [4, 128, 32, 512], P('section', 'rows'), may hold values from -6 to 6
- mirror_held: bfloat16 [4, 128, 32, 512], P('section', 'rows'), may hold values from -6 to 6
- target: bfloat16 [128, 32, 512], P('rows'), may hold values from -6 to 6
- w_first: bfloat16 [4, 3, 3, 512, 512], P('section'), may hold values from -0.09375 to 0.09375
- w_second: bfloat16 [4, 3, 3, 512, 512], P('section'), may hold values from -0.09375 to 0.09375
Outputs:
- fwd_next: bfloat16 [4, 128, 32, 512], P('section', 'rows')
- grad_next: bfloat16 [4, 128, 32, 512], P('section', 'rows')
- mirror_next: bfloat16 [4, 128, 32, 512], P('section', 'rows')
The draws below stay inside these ranges and needn't reach their ends.
All inputs are finite; a program needn't handle non-finite values.
Results may differ from the reference program's by a relative error of at most 0.0085.
Values may be sent and summed in bfloat16 or wider, within the bound.
A program may use at most 64 MiB of HBM per device.

```python
import jax
import jax.numpy as jnp
from jax import lax

C = 512
W = 32
SECTIONS = 4
H = 128


def block_scale(own_key, shape, pieces, least, top_value):
    level, own = 1.0, jax.random.fold_in(own_key, 6)
    for dim, blocks in pieces:
        draws = jnp.exp(jax.random.uniform(jax.random.fold_in(own, dim), (blocks,), jnp.float32, least / len(pieces), top_value / len(pieces)))
        level = level * jnp.repeat(draws, shape[dim] // blocks).reshape([-1 if axis == dim else 1 for axis in range(len(shape))])
    return level


def noise(stream_key, extent, width, limit, pieces=(), kind=jnp.bfloat16):
    result = jax.random.normal(stream_key, extent, jnp.float32) * width
    if len(pieces) > 0:
        result = block_scale(stream_key, extent, pieces, -0.22, 0.18) * result
    return jnp.clip(result, min=-limit, max=limit).astype(kind)


def setup_inputs(seed: int = 0) -> dict:
    key_of = jax.random.split(jax.random.key(seed), 8)
    fwd_in = noise(key_of[0], (SECTIONS, H, W, C), 1.0, 6.0, ((0, 4), (1, 8)))
    grad_in = noise(key_of[1], (SECTIONS, H, W, C), 1.0, 6.0, ((0, 4), (1, 8)))
    saved_in = noise(key_of[2], (SECTIONS, H, W, C), 1.0, 6.0, ((0, 4), (1, 8)))
    mirror_held = noise(key_of[3], (SECTIONS, H, W, C), 1.0, 6.0, ((0, 4), (1, 8)))
    target = noise(key_of[4], (H, W, C), 1.0, 6.0, ((0, 8),))
    w_first = noise(key_of[5], (SECTIONS, 3, 3, C, C), (9 * C) ** -0.5, 0.09375, ((0, 4),))
    w_second = noise(key_of[6], (SECTIONS, 3, 3, C, C), (9 * C) ** -0.5, 0.09375, ((0, 4),))
    return dict(fwd_in=fwd_in, grad_in=grad_in, saved_in=saved_in, mirror_held=mirror_held, target=target, w_first=w_first, w_second=w_second)


def conv_same(field, kernel):
    return lax.conv_general_dilated(field[None], kernel, (1, 1), ((1, 1), (1, 1)), dimension_numbers=("NHWC", "HWIO", "NHWC"), preferred_element_type=jnp.float32)[0]


def flipped(kernel):
    return jnp.transpose(kernel[::-1, ::-1], (0, 1, 3, 2))


def silu_slope(pre):
    sig = jax.nn.sigmoid(pre)
    return sig * (1.0 + pre * (1.0 - sig))


def reference(fwd_in, grad_in, saved_in, mirror_held, target, w_first, w_second):
    sections = fwd_in.shape[0]

    def one_section(items):
        index, act, grad, saved, held, kern_one, kern_two = items
        decoder = (index >= sections // 2).astype(jnp.float32)
        is_last = index == sections - 1
        block_in = act.astype(jnp.float32) + decoder * held.astype(jnp.float32)
        block_b = block_in.astype(jnp.bfloat16)
        hidden = jax.nn.silu(conv_same(block_b, kern_one)).astype(jnp.bfloat16)
        output = (block_in + conv_same(hidden, kern_two)).astype(jnp.bfloat16)
        g_top = jnp.where(is_last, output.astype(jnp.float32) - target.astype(jnp.float32), grad.astype(jnp.float32) + (1.0 - decoder) * held.astype(jnp.float32)).astype(jnp.bfloat16)
        kept = jnp.where(is_last, block_b, saved)
        pre = conv_same(kept, kern_one)
        g_mid = (silu_slope(pre) * conv_same(g_top, flipped(kern_two))).astype(jnp.bfloat16)
        g_low = (g_top.astype(jnp.float32) + conv_same(g_mid, flipped(kern_one))).astype(jnp.bfloat16)
        return output, g_low

    indices = jnp.arange(sections, dtype=jnp.int32)
    outputs, lows = lax.map(one_section, (indices, fwd_in, grad_in, saved_in, mirror_held, w_first, w_second))
    zero = jnp.zeros_like(outputs[:1])
    fwd_next = jnp.concatenate([zero, outputs[:-1]], axis=0)
    grad_next = jnp.concatenate([lows[1:], zero], axis=0)
    decoder_mask = (indices >= sections // 2)[:, None, None, None]
    mirror_next = jnp.where(decoder_mask, outputs[::-1], lows[::-1])
    return fwd_next, grad_next, mirror_next
```

```python
import functools

import jax
import jax.numpy as jnp
from jax import lax
from jax.experimental import pallas as pl
from jax.experimental.pallas import tpu as pltpu
from jax.sharding import PartitionSpec as P

MESH = pl.DeviceIdType.MESH
U, KEPT, GTOP, HID, GMID = range(5)
FWD, GRAD, MIRROR = range(3)


def relay_kernel(
    sections, row_devices, width, halves,
    act_hbm, grad_hbm, saved_hbm, held_hbm, target_hbm, w1_hbm, w2_hbm,
    fwd_out, grad_out, mirror_out,
    act, grad, held, target, w1, w2, field, slope, y, low, zeros,
    in_sem, halo_send, halo_recv, out_send, out_recv, local_sem,
):
    size, channels = act.shape
    part = channels // halves
    section = lax.axis_index("section")
    row = lax.axis_index("rows")
    half_sections = sections // 2
    decoder = section >= half_sections
    is_last = section == sections - 1
    dec = decoder.astype(jnp.float32)
    has_up, has_down = row > 0, row < row_devices - 1
    has_prev, has_next = section > 0, section < sections - 1
    mirror = sections - 1 - section
    middle_enc = section == half_sections - 1
    middle_dec = section == half_sections
    middle = jnp.logical_or(middle_enc, middle_dec)
    encoder = jnp.logical_not(decoder)
    inner_dec = jnp.logical_and(decoder, jnp.logical_not(is_last))
    others = jnp.logical_not(inner_dec)
    not_last = jnp.logical_not(is_last)
    at_up = (section, row - 1)
    at_down = (section, row + 1)
    at_prev = (section - 1, row)
    at_next = (section + 1, row)
    at_mirror = (mirror, row)

    inner = pl.ds(width, size)

    def load(src, dst, k):
        return pltpu.make_async_copy(src, dst, in_sem.at[k])

    load_act = load(act_hbm, act, 0)
    load_held = load(held_hbm, held, 1)
    load_grad = load(grad_hbm, grad, 2)
    load_saved = load(saved_hbm, field.at[KEPT, inner], 3)
    load_target = load(target_hbm, target, 4)
    load_w1 = load(w1_hbm, w1, 5)
    load_w2 = load(w2_hbm, w2, 6)
    for copy in (load_act, load_held, load_grad, load_saved, load_w1, load_target, load_w2):
        copy.start()

    barrier = pltpu.get_barrier_semaphore()
    partners = ((has_up, at_up), (has_down, at_down), (has_prev, at_prev), (has_next, at_next))
    count = jnp.int32(1)
    for cond, where in partners:
        @pl.when(cond)
        def _(where=where):
            pl.semaphore_signal(barrier, inc=1, device_id=where, device_id_type=MESH)
        count = count + cond.astype(jnp.int32)
    pl.semaphore_signal(barrier, inc=1, device_id=at_mirror, device_id_type=MESH)

    for k in range(5):
        @pl.when(jnp.logical_not(has_up))
        def _(k=k):
            field[k, pl.ds(0, width)] = jnp.zeros((width, channels), field.dtype)

        @pl.when(jnp.logical_not(has_down))
        def _(k=k):
            field[k, pl.ds(width + size, width)] = jnp.zeros((width, channels), field.dtype)

    load_act.wait()
    load_held.wait()
    field[U, inner] = (act[...].astype(jnp.float32) + dec * held[...].astype(jnp.float32)).astype(field.dtype)
    load_grad.wait()

    @pl.when(not_last)
    def _():
        top = grad[...].astype(jnp.float32) + (1.0 - dec) * held[...].astype(jnp.float32)
        field[GTOP, inner] = top.astype(field.dtype)

    load_saved.wait()
    pl.semaphore_wait(barrier, count)

    def halo_up(k):
        return pltpu.make_async_remote_copy(
            src_ref=field.at[k, pl.ds(width, width)],
            dst_ref=field.at[k, pl.ds(width + size, width)],
            send_sem=halo_send.at[k, 0],
            recv_sem=halo_recv.at[k, 0],
            device_id=at_up,
            device_id_type=MESH,
        )

    def halo_down(k):
        return pltpu.make_async_remote_copy(
            src_ref=field.at[k, pl.ds(size, width)],
            dst_ref=field.at[k, pl.ds(0, width)],
            send_sem=halo_send.at[k, 1],
            recv_sem=halo_recv.at[k, 1],
            device_id=at_down,
            device_id_type=MESH,
        )

    def send_halo(k):
        @pl.when(has_up)
        def _():
            halo_up(k).start()

        @pl.when(has_down)
        def _():
            halo_down(k).start()

    def wait_halo(k):
        @pl.when(has_up)
        def _():
            halo_up(k).wait_send()
            halo_down(k).wait_recv()

        @pl.when(has_down)
        def _():
            halo_down(k).wait_send()
            halo_up(k).wait_recv()

    send_halo(U)

    @pl.when(not_last)
    def _():
        send_halo(KEPT)
        send_halo(GTOP)

    out_refs = (fwd_out, grad_out, mirror_out)

    def zero_fill(kind):
        return pltpu.make_async_copy(zeros, out_refs[kind], local_sem.at[0])

    @pl.when(jnp.logical_not(has_prev))
    def _():
        zeros[...] = jnp.zeros_like(zeros)
        zero_fill(FWD).start()

    @pl.when(is_last)
    def _():
        zeros[...] = jnp.zeros_like(zeros)
        zero_fill(GRAD).start()

    def columns(n):
        return pl.ds(pl.multiple_of(n * part, part), part)

    def deliver(src, kind, n, where):
        return pltpu.make_async_remote_copy(
            src_ref=src.at[:, columns(n)],
            dst_ref=out_refs[kind].at[:, columns(n)],
            send_sem=out_send.at[kind, n],
            recv_sem=out_recv.at[kind, n],
            device_id=where,
            device_id_type=MESH,
        )

    def conv(k, w, flip, n):
        column = lax.broadcasted_iota(jnp.int32, (size, 1), 0) % width
        total = None
        for b in (0, 2, 1):
            partial = None
            for a in range(3):
                x = field[k, pl.ds(a * width, size)]
                if flip:
                    taps = w[3 * (2 - a) + 2 - b, columns(n), :]
                    dims = (((1,), (1,)), ((), ()))
                else:
                    taps = w[3 * a + b, :, columns(n)]
                    dims = (((1,), (0,)), ((), ()))
                term = lax.dot_general(x, taps, dims, preferred_element_type=jnp.float32)
                partial = term if partial is None else partial + term
            if b == 0:
                partial = jnp.where(column == 0, 0.0, pltpu.roll(partial, 1, 0))
            if b == 2:
                partial = jnp.where(column == width - 1, 0.0, pltpu.roll(partial, size - 1, 0))
            total = partial if total is None else total + partial
        return total

    def step_hidden():
        wait_halo(U)

        def body(n, _):
            value = conv(U, w1, False, n)
            sig = jax.nn.sigmoid(value)
            field[HID, inner, columns(n)] = (value * sig).astype(field.dtype)

            @pl.when(is_last)
            def _():
                slope[:, columns(n)] = sig * (1.0 + value * (1.0 - sig))
            return 0

        lax.fori_loop(0, halves, body, 0)
        send_halo(HID)

    def step_pre():
        wait_halo(KEPT)

        def body(n, _):
            value = conv(KEPT, w1, False, n)
            sig = jax.nn.sigmoid(value)
            slope[:, columns(n)] = sig * (1.0 + value * (1.0 - sig))
            return 0

        lax.fori_loop(0, halves, body, 0)

    def step_output():
        wait_halo(HID)

        def body(n, _):
            base = act[:, columns(n)].astype(jnp.float32) + dec * held[:, columns(n)].astype(jnp.float32)
            value = (base + conv(HID, w2, False, n)).astype(y.dtype)
            y[:, columns(n)] = value

            @pl.when(is_last)
            def _():
                top = value.astype(jnp.float32) - target[:, columns(n)].astype(jnp.float32)
                field[GTOP, inner, columns(n)] = top.astype(field.dtype)

            @pl.when(jnp.logical_and(encoder, jnp.logical_not(middle)))
            def _():
                deliver(y, MIRROR, n, at_mirror).start()

            @pl.when(has_next)
            def _():
                deliver(y, FWD, n, at_next).start()
            return 0

        lax.fori_loop(0, halves, body, 0)

        @pl.when(is_last)
        def _():
            send_halo(GTOP)

    def step_back():
        wait_halo(GTOP)

        def body(n, _):
            value = conv(GTOP, w2, True, n)
            field[GMID, inner, columns(n)] = (slope[:, columns(n)] * value).astype(field.dtype)
            return 0

        lax.fori_loop(0, halves, body, 0)
        send_halo(GMID)

    def step_low():
        wait_halo(GMID)

        def body(n, _):
            base = field[GTOP, inner, columns(n)].astype(jnp.float32)
            low[:, columns(n)] = (base + conv(GMID, w1, True, n)).astype(low.dtype)

            @pl.when(jnp.logical_and(decoder, jnp.logical_not(middle)))
            def _():
                deliver(low, MIRROR, n, at_mirror).start()

            @pl.when(has_prev)
            def _():
                deliver(low, GRAD, n, at_prev).start()
            return 0

        lax.fori_loop(0, halves, body, 0)

    load_w1.wait()
    pl.when(others)(step_hidden)
    pl.when(not_last)(step_pre)
    load_w2.wait()
    load_target.wait()
    pl.when(others)(step_output)
    step_back()
    pl.when(inner_dec)(step_hidden)
    step_low()
    pl.when(inner_dec)(step_output)

    def twin(kind):
        return pltpu.make_async_copy(out_refs[kind], mirror_out, local_sem.at[1])

    @pl.when(has_prev)
    def _():
        for n in range(halves):
            deliver(y, FWD, n, at_next).wait_recv()

    @pl.when(middle_dec)
    def _():
        twin(FWD).start()

    @pl.when(has_next)
    def _():
        for n in range(halves):
            deliver(low, GRAD, n, at_prev).wait_recv()

    @pl.when(middle_enc)
    def _():
        twin(GRAD).start()

    @pl.when(jnp.logical_not(middle))
    def _():
        for n in range(halves):
            deliver(y, MIRROR, n, at_mirror).wait_recv()
            deliver(y, MIRROR, n, at_mirror).wait_send()

    @pl.when(has_next)
    def _():
        for n in range(halves):
            deliver(y, FWD, n, at_next).wait_send()

    @pl.when(has_prev)
    def _():
        for n in range(halves):
            deliver(low, GRAD, n, at_prev).wait_send()

    @pl.when(jnp.logical_not(has_prev))
    def _():
        zero_fill(FWD).wait()

    @pl.when(is_last)
    def _():
        zero_fill(GRAD).wait()

    @pl.when(middle)
    def _():
        twin(FWD).wait()


def on_device(fwd_in, grad_in, saved_in, mirror_held, target, w_first, w_second):
    _, rows, width, channels = fwd_in.shape
    size = rows * width
    taps = w_first.shape[1] * w_first.shape[2]
    halves = 2
    dtype = fwd_in.dtype
    sections = lax.axis_size("section")
    row_devices = lax.axis_size("rows")
    flat = lambda value: value.reshape(size, channels)
    flat_w = lambda value: value.reshape(taps, channels, channels)
    any_spec = pl.BlockSpec(memory_space=pl.ANY)
    plane = pltpu.VMEM((size, channels), dtype)
    weight = pltpu.VMEM((taps, channels, channels), dtype)
    outs = pl.pallas_call(
        functools.partial(relay_kernel, sections, row_devices, width, halves),
        out_shape=[jax.ShapeDtypeStruct((size, channels), dtype)] * 3,
        in_specs=[any_spec] * 7,
        out_specs=[any_spec] * 3,
        scratch_shapes=[
            plane, plane, plane, plane,
            weight, weight,
            pltpu.VMEM((5, size + 2 * width, channels), dtype),
            pltpu.VMEM((size, channels), jnp.float32),
            plane, plane, plane,
            pltpu.SemaphoreType.DMA((7,)),
            pltpu.SemaphoreType.DMA((5, 2)),
            pltpu.SemaphoreType.DMA((5, 2)),
            pltpu.SemaphoreType.DMA((3, halves)),
            pltpu.SemaphoreType.DMA((3, halves)),
            pltpu.SemaphoreType.DMA((2,)),
        ],
        compiler_params=pltpu.CompilerParams(
            collective_id=0, has_side_effects=True, vmem_limit_bytes=48 * 2**20
        ),
        cost_estimate=pl.CostEstimate(
            flops=10 * size * taps * channels * channels,
            bytes_accessed=4 * taps * channels * channels + 16 * size * channels,
            transcendentals=2 * size * channels,
        ),
    )(
        flat(fwd_in), flat(grad_in), flat(saved_in), flat(mirror_held), flat(target),
        flat_w(w_first), flat_w(w_second),
    )
    return tuple(value.reshape(fwd_in.shape) for value in outs)


def solution(mesh):
    blocks = P("section", "rows", None, None)
    weights = P("section", None, None, None, None)
    return jax.shard_map(
        on_device,
        mesh=mesh,
        in_specs=(blocks, blocks, blocks, blocks, P("rows", None, None), weights, weights),
        out_specs=(blocks, blocks, blocks),
        check_vma=False,
    )
```

```python
import functools

import jax
import jax.numpy as jnp
from jax import lax
from jax.experimental import pallas as pl
from jax.experimental.pallas import tpu as pltpu
from jax.sharding import PartitionSpec as P

MESH = pl.DeviceIdType.MESH
U, KEPT, GTOP, HID, GMID = range(5)
FWD, GRAD, MIRROR = range(3)
HALVES = 2


def relay_kernel(
    sections, row_devices, width, chunks,
    act_hbm, grad_hbm, saved_hbm, held_hbm, target_hbm, w1_hbm, w2_hbm,
    fwd_out, grad_out, mirror_out,
    act, grad, held, target, w1, w2, field, slope, y, low,
    in_sem, w_sem, halo_send, halo_recv, out_send, out_recv,
):
    size, channels = act.shape
    part = channels // HALVES
    section = lax.axis_index("section")
    row = lax.axis_index("rows")
    half_sections = sections // 2
    decoder = section >= half_sections
    is_last = section == sections - 1
    dec = decoder.astype(jnp.float32)
    has_up, has_down = row > 0, row < row_devices - 1
    has_prev, has_next = section > 0, section < sections - 1
    mirror = sections - 1 - section
    middle_enc = section == half_sections - 1
    middle_dec = section == half_sections
    middle = jnp.logical_or(middle_enc, middle_dec)
    encoder = jnp.logical_not(decoder)
    inner_dec = jnp.logical_and(decoder, jnp.logical_not(is_last))
    others = jnp.logical_not(inner_dec)
    not_last = jnp.logical_not(is_last)
    at_up = (section, row - 1)
    at_down = (section, row + 1)
    at_prev = (section - 1, row)
    at_next = (section + 1, row)
    at_mirror = (mirror, row)

    inner = pl.ds(width, size)

    def load(src, dst, k):
        return pltpu.make_async_copy(src, dst, in_sem.at[k])

    load_act = load(act_hbm, act, 0)
    load_held = load(held_hbm, held, 1)
    load_grad = load(grad_hbm, grad, 2)
    load_saved = load(saved_hbm, field.at[KEPT, inner], 3)
    load_target = load(target_hbm, target, 4)

    def load_tap(j, a, b):
        t = 3 * a + b
        src, dst = ((w1_hbm, w1), (w2_hbm, w2))[j]
        return pltpu.make_async_copy(src.at[t], dst.at[t], w_sem.at[j, t])

    taps = [(a, b) for a in (1, 0, 2) for b in (0, 2, 1)]
    for copy in (load_act, load_held, load_saved):
        copy.start()
    for a, b in taps:
        load_tap(0, a, b).start()
    for copy in (load_grad, load_target):
        copy.start()

    barrier = pltpu.get_barrier_semaphore()
    partners = ((has_up, at_up), (has_down, at_down), (has_prev, at_prev), (has_next, at_next))
    count = jnp.int32(1)
    for cond, where in partners:
        @pl.when(cond)
        def _(where=where):
            pl.semaphore_signal(barrier, inc=1, device_id=where, device_id_type=MESH)
        count = count + cond.astype(jnp.int32)
    pl.semaphore_signal(barrier, inc=1, device_id=at_mirror, device_id_type=MESH)

    for k in range(5):
        @pl.when(jnp.logical_not(has_up))
        def _(k=k):
            field[k, pl.ds(0, width)] = jnp.zeros((width, channels), field.dtype)

        @pl.when(jnp.logical_not(has_down))
        def _(k=k):
            field[k, pl.ds(width + size, width)] = jnp.zeros((width, channels), field.dtype)

    def columns(n):
        return pl.ds(n * part, part)

    def halo_up(k, n):
        return pltpu.make_async_remote_copy(
            src_ref=field.at[k, pl.ds(width, width), columns(n)],
            dst_ref=field.at[k, pl.ds(width + size, width), columns(n)],
            send_sem=halo_send.at[k, 0, n],
            recv_sem=halo_recv.at[k, 0, n],
            device_id=at_up,
            device_id_type=MESH,
        )

    def halo_down(k, n):
        return pltpu.make_async_remote_copy(
            src_ref=field.at[k, pl.ds(size, width), columns(n)],
            dst_ref=field.at[k, pl.ds(0, width), columns(n)],
            send_sem=halo_send.at[k, 1, n],
            recv_sem=halo_recv.at[k, 1, n],
            device_id=at_down,
            device_id_type=MESH,
        )

    def send_halo(k, n):
        @pl.when(has_up)
        def _():
            halo_up(k, n).start()

        @pl.when(has_down)
        def _():
            halo_down(k, n).start()

    def wait_halo(k):
        @pl.when(has_up)
        def _():
            for n in range(HALVES):
                halo_up(k, n).wait_send()
                halo_down(k, n).wait_recv()

        @pl.when(has_down)
        def _():
            for n in range(HALVES):
                halo_down(k, n).wait_send()
                halo_up(k, n).wait_recv()

    load_act.wait()
    load_held.wait()
    field[U, inner] = (act[...].astype(jnp.float32) + dec * held[...].astype(jnp.float32)).astype(field.dtype)
    pl.semaphore_wait(barrier, count)
    for n in range(HALVES):
        send_halo(U, n)
    load_saved.wait()
    load_grad.wait()

    @pl.when(not_last)
    def _():
        for n in range(HALVES):
            send_halo(KEPT, n)
        top = grad[...].astype(jnp.float32) + (1.0 - dec) * held[...].astype(jnp.float32)
        field[GTOP, inner] = top.astype(field.dtype)
        for n in range(HALVES):
            send_halo(GTOP, n)

    for a, b in taps:
        load_tap(1, a, b).start()

    out_refs = (fwd_out, grad_out, mirror_out)

    def deliver(src, kind, c, where):
        n, first, count = chunks[c]
        at = (pl.ds(first, count), columns(n))
        return pltpu.make_async_remote_copy(
            src_ref=src.at[at],
            dst_ref=out_refs[kind].at[at],
            send_sem=out_send.at[kind, c],
            recv_sem=out_recv.at[kind, c],
            device_id=where,
            device_id_type=MESH,
        )

    def conv(k, w, flip, n, first=0, count=size, fresh=False, arrive=None):
        column = lax.broadcasted_iota(jnp.int32, (count, 1), 0) % width
        total = None
        for group in ((1,), (0, 2)) if fresh else ((1, 0, 2),):
            if fresh and 0 in group:
                wait_halo(k)
            for b in (0, 2, 1):
                partial = None
                for a in group:
                    if arrive is not None:
                        arrive(a, b)
                    x = field[k, pl.ds(first + a * width, count)]
                    if flip:
                        tap = w[3 * (2 - a) + 2 - b, columns(n), :]
                        dims = (((1,), (1,)), ((), ()))
                    else:
                        tap = w[3 * a + b, :, columns(n)]
                        dims = (((1,), (0,)), ((), ()))
                    term = lax.dot_general(x, tap, dims, preferred_element_type=jnp.float32)
                    partial = term if partial is None else partial + term
                if b == 0:
                    partial = jnp.where(column == 0, 0.0, pltpu.roll(partial, 1, 0))
                if b == 2:
                    partial = jnp.where(column == width - 1, 0.0, pltpu.roll(partial, count - 1, 0))
                total = partial if total is None else total + partial
        return total

    def first_tap(a, b):
        load_tap(0, a, b).wait()

    def step_hidden(arrive=None):
        for n in range(HALVES):
            value = conv(U, w1, False, n, fresh=n == 0, arrive=arrive if n == 0 else None)
            sig = jax.nn.sigmoid(value)
            field[HID, inner, columns(n)] = (value * sig).astype(field.dtype)
            send_halo(HID, n)

            @pl.when(is_last)
            def _():
                slope[:, columns(n)] = sig * (1.0 + value * (1.0 - sig))

    def step_pre(arrive=None):
        for n in range(HALVES):
            value = conv(KEPT, w1, False, n, fresh=n == 0, arrive=arrive if n == 0 else None)
            sig = jax.nn.sigmoid(value)
            slope[:, columns(n)] = sig * (1.0 + value * (1.0 - sig))

    def step_output():
        for c, (n, first, count) in enumerate(chunks):
            at = (pl.ds(first, count), columns(n))
            base = act[at].astype(jnp.float32) + dec * held[at].astype(jnp.float32)
            value = (base + conv(HID, w2, False, n, first, count, fresh=c == 0)).astype(y.dtype)
            y[at] = value

            @pl.when(is_last)
            def _():
                top = value.astype(jnp.float32) - target[at].astype(jnp.float32)
                field[GTOP, pl.ds(width + first, count), columns(n)] = top.astype(field.dtype)
                if first + count == size:
                    send_halo(GTOP, n)

            @pl.when(jnp.logical_and(encoder, jnp.logical_not(middle)))
            def _():
                deliver(y, MIRROR, c, at_mirror).start()

            @pl.when(has_next)
            def _():
                deliver(y, FWD, c, at_next).start()

    def step_back():
        for n in range(HALVES):
            value = conv(GTOP, w2, True, n, fresh=n == 0)
            field[GMID, inner, columns(n)] = (slope[:, columns(n)] * value).astype(field.dtype)
            send_halo(GMID, n)

    def step_low():
        for c, (n, first, count) in enumerate(chunks):
            at = (pl.ds(first, count), columns(n))
            base = field[GTOP, pl.ds(width + first, count), columns(n)].astype(jnp.float32)
            low[at] = (base + conv(GMID, w1, True, n, first, count, fresh=c == 0)).astype(low.dtype)

            @pl.when(jnp.logical_and(decoder, jnp.logical_not(middle)))
            def _():
                deliver(low, MIRROR, c, at_mirror).start()

            @pl.when(has_prev)
            def _():
                deliver(low, GRAD, c, at_prev).start()

    pl.when(others)(lambda: step_hidden(first_tap))
    pl.when(inner_dec)(lambda: step_pre(first_tap))
    pl.when(encoder)(step_pre)
    load_target.wait()
    for a, b in taps:
        load_tap(1, a, b).wait()
    pl.when(others)(step_output)
    step_back()
    step_low()
    pl.when(inner_dec)(step_hidden)
    pl.when(inner_dec)(step_output)

    def drain(cond, src, kind, where, sent):
        @pl.when(cond)
        def _():
            for c in range(len(chunks)):
                copy = deliver(src, kind, c, where)
                (copy.wait_send if sent else copy.wait_recv)()

    apart = jnp.logical_not(middle)
    drain(has_prev, y, FWD, at_next, False)
    drain(has_next, low, GRAD, at_prev, False)
    drain(apart, y, MIRROR, at_mirror, False)
    drain(has_next, y, FWD, at_next, True)
    drain(has_prev, low, GRAD, at_prev, True)
    drain(apart, y, MIRROR, at_mirror, True)


def finish_kernel(sections, pieces, fwd, grad, mirror, fwd_out, grad_out, mirror_out, zeros, sem):
    section = lax.axis_index("section")
    size = zeros.shape[0]
    piece = size // pieces
    is_first, is_last = section == 0, section == sections - 1
    middle_enc = section == sections // 2 - 1
    middle_dec = section == sections // 2
    apart = jnp.logical_not(jnp.logical_or(middle_enc, middle_dec))
    moves = (
        (jnp.logical_not(is_first), fwd, fwd_out, 0),
        (is_first, zeros, fwd_out, 0),
        (jnp.logical_not(is_last), grad, grad_out, 1),
        (is_last, zeros, grad_out, 1),
        (middle_dec, fwd, mirror_out, 2),
        (middle_enc, grad, mirror_out, 2),
        (apart, mirror, mirror_out, 2),
    )

    def copies(src, dst, k):
        for p in range(pieces):
            rows = pl.ds(p * piece, piece)
            yield pltpu.make_async_copy(src.at[rows], dst.at[rows], sem.at[k, p])

    @pl.when(jnp.logical_or(is_first, is_last))
    def _():
        zeros[...] = jnp.zeros_like(zeros)

    for cond, src, dst, k in moves:
        @pl.when(cond)
        def _(src=src, dst=dst, k=k):
            for copy in copies(src, dst, k):
                copy.start()
    for dst, k in ((fwd_out, 0), (grad_out, 1), (mirror_out, 2)):
        for copy in copies(zeros, dst, k):
            copy.wait()


def on_device(fwd_in, grad_in, saved_in, mirror_held, target, w_first, w_second):
    _, rows, width, channels = fwd_in.shape
    size = rows * width
    taps = w_first.shape[1] * w_first.shape[2]
    chunks = ((0, 0, size), (1, 0, size // 2), (1, size // 2, size // 2))
    dtype = fwd_in.dtype
    sections = lax.axis_size("section")
    row_devices = lax.axis_size("rows")
    flat = lambda value: value.reshape(size, channels)
    flat_w = lambda value: value.reshape(taps, channels, channels)
    any_spec = pl.BlockSpec(memory_space=pl.ANY)
    hbm_spec = pl.BlockSpec(memory_space=pltpu.HBM)
    plane = pltpu.VMEM((size, channels), dtype)
    weight = pltpu.VMEM((taps, channels, channels), dtype)
    outs = pl.pallas_call(
        functools.partial(relay_kernel, sections, row_devices, width, chunks),
        out_shape=[jax.ShapeDtypeStruct((size, channels), dtype)] * 3,
        in_specs=[hbm_spec] * 7,
        out_specs=[any_spec] * 3,
        scratch_shapes=[
            plane, plane, plane, plane,
            weight, weight,
            pltpu.VMEM((5, size + 2 * width, channels), dtype),
            pltpu.VMEM((size, channels), jnp.float32),
            plane, plane,
            pltpu.SemaphoreType.DMA((5,)),
            pltpu.SemaphoreType.DMA((2, taps)),
            pltpu.SemaphoreType.DMA((5, 2, HALVES)),
            pltpu.SemaphoreType.DMA((5, 2, HALVES)),
            pltpu.SemaphoreType.DMA((3, len(chunks))),
            pltpu.SemaphoreType.DMA((3, len(chunks))),
        ],
        compiler_params=pltpu.CompilerParams(
            collective_id=0, has_side_effects=True, vmem_limit_bytes=62 * 2**20
        ),
        cost_estimate=pl.CostEstimate(
            flops=10 * size * taps * channels * channels,
            bytes_accessed=4 * taps * channels * channels + 16 * size * channels,
            transcendentals=2 * size * channels,
        ),
    )(
        flat(fwd_in), flat(grad_in), flat(saved_in), flat(mirror_held), flat(target),
        flat_w(w_first), flat_w(w_second),
    )
    pieces = 2
    outs = pl.pallas_call(
        functools.partial(finish_kernel, sections, pieces),
        out_shape=[jax.ShapeDtypeStruct((size, channels), dtype)] * 3,
        in_specs=[any_spec] * 3,
        out_specs=[hbm_spec] * 3,
        scratch_shapes=[plane, pltpu.SemaphoreType.DMA((3, pieces))],
        compiler_params=pltpu.CompilerParams(vmem_limit_bytes=62 * 2**20),
    )(*outs)
    return tuple(value.reshape(fwd_in.shape) for value in outs)


def solution(mesh):
    blocks = P("section", "rows", None, None)
    weights = P("section", None, None, None, None)
    return jax.shard_map(
        on_device,
        mesh=mesh,
        in_specs=(blocks, blocks, blocks, blocks, P("rows", None, None), weights, weights),
        out_specs=(blocks, blocks, blocks),
        check_vma=False,
    )
```

```python
import functools

import jax
import jax.numpy as jnp
from jax import lax
from jax.experimental import pallas as pl
from jax.experimental.pallas import tpu as pltpu
from jax.sharding import PartitionSpec as P

MESH = pl.DeviceIdType.MESH
U, KEPT, GTOP, HID, GMID = range(5)
FWD, GRAD, MIRROR = range(3)
HALVES = 2


def relay_kernel(
    sections, row_devices, width, chunks,
    act_hbm, grad_hbm, saved_hbm, held_hbm, target_hbm, w1_hbm, w2_hbm,
    fwd_out, grad_out, mirror_out,
    act, grad, held, target, w1, w2, field, slope, y, low,
    in_sem, w_sem, halo_send, halo_recv, out_send, out_recv,
):
    size, channels = act.shape
    part = channels // HALVES
    section = lax.axis_index("section")
    row = lax.axis_index("rows")
    half_sections = sections // 2
    decoder = section >= half_sections
    is_last = section == sections - 1
    dec = decoder.astype(jnp.float32)
    has_up, has_down = row > 0, row < row_devices - 1
    has_prev, has_next = section > 0, section < sections - 1
    mirror = sections - 1 - section
    middle_enc = section == half_sections - 1
    middle_dec = section == half_sections
    middle = jnp.logical_or(middle_enc, middle_dec)
    encoder = jnp.logical_not(decoder)
    inner_dec = jnp.logical_and(decoder, jnp.logical_not(is_last))
    others = jnp.logical_not(inner_dec)
    not_last = jnp.logical_not(is_last)
    at_up = (section, row - 1)
    at_down = (section, row + 1)
    at_prev = (section - 1, row)
    at_next = (section + 1, row)
    at_mirror = (mirror, row)

    inner = pl.ds(width, size)

    def load(src, dst, k):
        return pltpu.make_async_copy(src, dst, in_sem.at[k])

    load_act = load(act_hbm, act, 0)
    load_held = load(held_hbm, held, 1)
    load_grad = load(grad_hbm, grad, 2)
    load_saved = load(saved_hbm, field.at[KEPT, inner], 3)
    load_target = load(target_hbm, target, 4)

    def load_tap(j, a, b):
        t = 3 * a + b
        src, dst = ((w1_hbm, w1), (w2_hbm, w2))[j]
        return pltpu.make_async_copy(src.at[t], dst.at[t], w_sem.at[j, t])

    taps = [(a, b) for a in (1, 2, 0) for b in range(3)]
    for copy in (load_act, load_held, load_saved):
        copy.start()
    for a, b in taps:
        load_tap(0, a, b).start()
    for copy in (load_grad, load_target):
        copy.start()

    barrier = pltpu.get_barrier_semaphore()
    partners = ((has_up, at_up), (has_down, at_down), (has_prev, at_prev), (has_next, at_next))
    count = jnp.int32(1)
    for cond, where in partners:
        @pl.when(cond)
        def _(where=where):
            pl.semaphore_signal(barrier, inc=1, device_id=where, device_id_type=MESH)
        count = count + cond.astype(jnp.int32)
    pl.semaphore_signal(barrier, inc=1, device_id=at_mirror, device_id_type=MESH)

    for k in range(5):
        @pl.when(jnp.logical_not(has_up))
        def _(k=k):
            field[k, pl.ds(0, width)] = jnp.zeros((width, channels), field.dtype)

        @pl.when(jnp.logical_not(has_down))
        def _(k=k):
            field[k, pl.ds(width + size, width)] = jnp.zeros((width, channels), field.dtype)

    def columns(n):
        return pl.ds(n * part, part)

    def halo_up(k, n):
        return pltpu.make_async_remote_copy(
            src_ref=field.at[k, pl.ds(width, width), columns(n)],
            dst_ref=field.at[k, pl.ds(width + size, width), columns(n)],
            send_sem=halo_send.at[k, 0, n],
            recv_sem=halo_recv.at[k, 0, n],
            device_id=at_up,
            device_id_type=MESH,
        )

    def halo_down(k, n):
        return pltpu.make_async_remote_copy(
            src_ref=field.at[k, pl.ds(size, width), columns(n)],
            dst_ref=field.at[k, pl.ds(0, width), columns(n)],
            send_sem=halo_send.at[k, 1, n],
            recv_sem=halo_recv.at[k, 1, n],
            device_id=at_down,
            device_id_type=MESH,
        )

    def send_halo(k, n):
        @pl.when(has_up)
        def _():
            halo_up(k, n).start()

        @pl.when(has_down)
        def _():
            halo_down(k, n).start()

    def wait_halo(k):
        @pl.when(has_up)
        def _():
            for n in range(HALVES):
                halo_up(k, n).wait_send()
                halo_down(k, n).wait_recv()

        @pl.when(has_down)
        def _():
            for n in range(HALVES):
                halo_down(k, n).wait_send()
                halo_up(k, n).wait_recv()

    load_act.wait()
    load_held.wait()
    field[U, inner] = (act[...].astype(jnp.float32) + dec * held[...].astype(jnp.float32)).astype(field.dtype)
    pl.semaphore_wait(barrier, count)
    for n in range(HALVES):
        send_halo(U, n)
    load_saved.wait()
    load_grad.wait()

    @pl.when(not_last)
    def _():
        for n in range(HALVES):
            send_halo(KEPT, n)
        top = grad[...].astype(jnp.float32) + (1.0 - dec) * held[...].astype(jnp.float32)
        field[GTOP, inner] = top.astype(field.dtype)
        for n in range(HALVES):
            send_halo(GTOP, n)

    for a, b in taps:
        load_tap(1, a, b).start()

    out_refs = (fwd_out, grad_out, mirror_out)

    def deliver(src, kind, c, where):
        n, first, count = chunks[c]
        at = (pl.ds(first, count), columns(n))
        return pltpu.make_async_remote_copy(
            src_ref=src.at[at],
            dst_ref=out_refs[kind].at[at],
            send_sem=out_send.at[kind, c],
            recv_sem=out_recv.at[kind, c],
            device_id=where,
            device_id_type=MESH,
        )

    def product(k, w, flip, b, group, n, first, count):
        x = [field[k, pl.ds(first + a * width, count)] for a in group]
        if flip:
            tap = [w[3 * (2 - a) + 2 - b, columns(n), :] for a in group]
            dims = (((1,), (1,)), ((), ()))
        else:
            tap = [w[3 * a + b, :, columns(n)] for a in group]
            dims = (((1,), (0,)), ((), ()))
        if len(group) > 1:
            x, tap = jnp.concatenate(x, 1), jnp.concatenate(tap, 1 if flip else 0)
        else:
            x, tap = x[0], tap[0]
        return lax.dot_general(x, tap, dims, preferred_element_type=jnp.float32)

    def partials(k, w, flip, n, first, count, fresh=False, arrive=None):
        groups = ((1, 2), (0,)) if fresh else ((0, 1, 2),)
        out = None
        for group in groups:
            if fresh and 0 in group:
                wait_halo(k)
            if arrive is not None:
                for b in range(3):
                    for a in group:
                        arrive(a, b)
            terms = [product(k, w, flip, b, group, n, first, count) for b in range(3)]
            out = terms if out is None else [p + q for p, q in zip(out, terms)]
        return out

    def merged(parts):
        left, centre, right = parts
        count = centre.shape[0]
        column = lax.broadcasted_iota(jnp.int32, (count, 1), 0) % width
        left = jnp.where(column == 0, 0.0, pltpu.roll(left, 1, 0))
        right = jnp.where(column == width - 1, 0.0, pltpu.roll(right, count - 1, 0))
        return left + centre + right

    def run(k, w, flip, store, send=None, arrive=None):
        waiting = None

        def flush(c, parts):
            n, first, count = chunks[c]
            store(n, first, count, merged(parts))

        for c, (n, first, count) in enumerate(chunks):
            parts = partials(k, w, flip, n, first, count, c == 0, arrive if c == 0 else None)
            if waiting is not None:
                flush(*waiting)
                if send is not None:
                    send(waiting[0])
            waiting = (c, parts)
        flush(*waiting)
        if send is not None:
            send(waiting[0])

    def first_tap(a, b):
        load_tap(0, a, b).wait()

    def halo_after(k):
        def send(c):
            n, first, count = chunks[c]
            if first + count == size:
                send_halo(k, n)
        return send

    def body(first, count):
        return pl.ds(width + first, count)

    def step_hidden(arrive=None):
        def store(n, first, count, value):
            sig = jax.nn.sigmoid(value)
            field[HID, body(first, count), columns(n)] = (value * sig).astype(field.dtype)
            slope[pl.ds(first, count), columns(n)] = sig * (1.0 + value * (1.0 - sig))

        run(U, w1, False, store, halo_after(HID), arrive)

    def step_pre(arrive=None):
        def store(n, first, count, value):
            sig = jax.nn.sigmoid(value)
            slope[pl.ds(first, count), columns(n)] = sig * (1.0 + value * (1.0 - sig))

        run(KEPT, w1, False, store, None, arrive)

    def step_output():
        def store(n, first, count, value):
            at = (pl.ds(first, count), columns(n))
            base = act[at].astype(jnp.float32) + dec * held[at].astype(jnp.float32)
            y[at] = (base + value).astype(y.dtype)

        def send(c):
            n, first, count = chunks[c]

            @pl.when(is_last)
            def _():
                at = (pl.ds(first, count), columns(n))
                top = y[at].astype(jnp.float32) - target[at].astype(jnp.float32)
                field[GTOP, body(first, count), columns(n)] = top.astype(field.dtype)
                if first + count == size:
                    send_halo(GTOP, n)

            @pl.when(jnp.logical_and(encoder, jnp.logical_not(middle)))
            def _():
                deliver(y, MIRROR, c, at_mirror).start()

            @pl.when(has_next)
            def _():
                deliver(y, FWD, c, at_next).start()

        run(HID, w2, False, store, send)

    def step_back():
        def store(n, first, count, value):
            at = (pl.ds(first, count), columns(n))
            field[GMID, body(first, count), columns(n)] = (slope[at] * value).astype(field.dtype)

        run(GTOP, w2, True, store, halo_after(GMID))

    def step_low():
        def store(n, first, count, value):
            base = field[GTOP, body(first, count), columns(n)].astype(jnp.float32)
            low[pl.ds(first, count), columns(n)] = (base + value).astype(low.dtype)

        def send(c):
            @pl.when(jnp.logical_and(decoder, jnp.logical_not(middle)))
            def _():
                deliver(low, MIRROR, c, at_mirror).start()

            @pl.when(has_prev)
            def _():
                deliver(low, GRAD, c, at_prev).start()

        run(GMID, w1, True, store, send)

    pl.when(others)(lambda: step_hidden(first_tap))
    pl.when(inner_dec)(lambda: step_pre(first_tap))
    pl.when(encoder)(step_pre)
    load_target.wait()
    for a, b in taps:
        load_tap(1, a, b).wait()
    pl.when(others)(step_output)
    step_back()
    step_low()
    pl.when(inner_dec)(step_hidden)
    pl.when(inner_dec)(step_output)

    def drain(cond, src, kind, where, sent):
        @pl.when(cond)
        def _():
            for c in range(len(chunks)):
                copy = deliver(src, kind, c, where)
                (copy.wait_send if sent else copy.wait_recv)()

    apart = jnp.logical_not(middle)
    drain(has_prev, y, FWD, at_next, False)
    drain(has_next, low, GRAD, at_prev, False)
    drain(apart, y, MIRROR, at_mirror, False)
    drain(has_next, y, FWD, at_next, True)
    drain(has_prev, low, GRAD, at_prev, True)
    drain(apart, y, MIRROR, at_mirror, True)


def finish_kernel(sections, pieces, fwd, grad, mirror, fwd_out, grad_out, mirror_out, zeros, sem):
    section = lax.axis_index("section")
    size = zeros.shape[0]
    piece = size // pieces
    is_first, is_last = section == 0, section == sections - 1
    middle_enc = section == sections // 2 - 1
    middle_dec = section == sections // 2
    apart = jnp.logical_not(jnp.logical_or(middle_enc, middle_dec))
    moves = (
        (jnp.logical_not(is_first), fwd, fwd_out, 0),
        (is_first, zeros, fwd_out, 0),
        (jnp.logical_not(is_last), grad, grad_out, 1),
        (is_last, zeros, grad_out, 1),
        (middle_dec, fwd, mirror_out, 2),
        (middle_enc, grad, mirror_out, 2),
        (apart, mirror, mirror_out, 2),
    )

    def copies(src, dst, k):
        for p in range(pieces):
            rows = pl.ds(p * piece, piece)
            yield pltpu.make_async_copy(src.at[rows], dst.at[rows], sem.at[k, p])

    @pl.when(jnp.logical_or(is_first, is_last))
    def _():
        zeros[...] = jnp.zeros_like(zeros)

    for cond, src, dst, k in moves:
        @pl.when(cond)
        def _(src=src, dst=dst, k=k):
            for copy in copies(src, dst, k):
                copy.start()
    for dst, k in ((fwd_out, 0), (grad_out, 1), (mirror_out, 2)):
        for copy in copies(zeros, dst, k):
            copy.wait()


def on_device(fwd_in, grad_in, saved_in, mirror_held, target, w_first, w_second):
    _, rows, width, channels = fwd_in.shape
    size = rows * width
    taps = w_first.shape[1] * w_first.shape[2]
    half = size // 2
    chunks = tuple((n, first, half) for n in range(HALVES) for first in (0, half))
    dtype = fwd_in.dtype
    sections = lax.axis_size("section")
    row_devices = lax.axis_size("rows")
    flat = lambda value: value.reshape(size, channels)
    flat_w = lambda value: value.reshape(taps, channels, channels)
    any_spec = pl.BlockSpec(memory_space=pl.ANY)
    hbm_spec = pl.BlockSpec(memory_space=pltpu.HBM)
    plane = pltpu.VMEM((size, channels), dtype)
    weight = pltpu.VMEM((taps, channels, channels), dtype)
    outs = pl.pallas_call(
        functools.partial(relay_kernel, sections, row_devices, width, chunks),
        out_shape=[jax.ShapeDtypeStruct((size, channels), dtype)] * 3,
        in_specs=[hbm_spec] * 7,
        out_specs=[any_spec] * 3,
        scratch_shapes=[
            plane, plane, plane, plane,
            weight, weight,
            pltpu.VMEM((5, size + 2 * width, channels), dtype),
            pltpu.VMEM((size, channels), jnp.float32),
            plane, plane,
            pltpu.SemaphoreType.DMA((5,)),
            pltpu.SemaphoreType.DMA((2, taps)),
            pltpu.SemaphoreType.DMA((5, 2, HALVES)),
            pltpu.SemaphoreType.DMA((5, 2, HALVES)),
            pltpu.SemaphoreType.DMA((3, len(chunks))),
            pltpu.SemaphoreType.DMA((3, len(chunks))),
        ],
        compiler_params=pltpu.CompilerParams(
            collective_id=0, has_side_effects=True, vmem_limit_bytes=62 * 2**20
        ),
        cost_estimate=pl.CostEstimate(
            flops=10 * size * taps * channels * channels,
            bytes_accessed=4 * taps * channels * channels + 16 * size * channels,
            transcendentals=2 * size * channels,
        ),
    )(
        flat(fwd_in), flat(grad_in), flat(saved_in), flat(mirror_held), flat(target),
        flat_w(w_first), flat_w(w_second),
    )
    pieces = 2
    outs = pl.pallas_call(
        functools.partial(finish_kernel, sections, pieces),
        out_shape=[jax.ShapeDtypeStruct((size, channels), dtype)] * 3,
        in_specs=[pl.BlockSpec(memory_space=pltpu.VMEM)] * 3,
        out_specs=[hbm_spec] * 3,
        scratch_shapes=[plane, pltpu.SemaphoreType.DMA((3, pieces))],
        compiler_params=pltpu.CompilerParams(vmem_limit_bytes=62 * 2**20),
    )(*outs)
    return tuple(value.reshape(fwd_in.shape) for value in outs)


def solution(mesh):
    blocks = P("section", "rows", None, None)
    weights = P("section", None, None, None, None)
    return jax.shard_map(
        on_device,
        mesh=mesh,
        in_specs=(blocks, blocks, blocks, blocks, P("rows", None, None), weights, weights),
        out_specs=(blocks, blocks, blocks),
        check_vma=False,
    )
```

```python
import functools

import jax
import jax.numpy as jnp
from jax import lax
from jax.experimental import pallas as pl
from jax.experimental.pallas import tpu as pltpu
from jax.sharding import PartitionSpec as P

MESH = pl.DeviceIdType.MESH
U, KEPT, GTOP, HID, GMID = range(5)
FWD, GRAD, MIRROR = range(3)
HALVES = 2


def relay_kernel(
    sections, row_devices, width,
    act_hbm, grad_hbm, saved_hbm, held_hbm, target_hbm, w1_hbm, w2_hbm,
    fwd_out, grad_out, mirror_out,
    act, grad, held, target, w1, w2, field, slope, y, low,
    in_sem, halo_send, halo_recv, out_send, out_recv,
):
    size, channels = act.shape
    part = channels // HALVES
    section = lax.axis_index("section")
    row = lax.axis_index("rows")
    half_sections = sections // 2
    decoder = section >= half_sections
    is_last = section == sections - 1
    dec = decoder.astype(jnp.float32)
    has_up, has_down = row > 0, row < row_devices - 1
    has_prev, has_next = section > 0, section < sections - 1
    mirror = sections - 1 - section
    middle_enc = section == half_sections - 1
    middle_dec = section == half_sections
    middle = jnp.logical_or(middle_enc, middle_dec)
    encoder = jnp.logical_not(decoder)
    inner_dec = jnp.logical_and(decoder, jnp.logical_not(is_last))
    others = jnp.logical_not(inner_dec)
    not_last = jnp.logical_not(is_last)
    at_up = (section, row - 1)
    at_down = (section, row + 1)
    at_prev = (section - 1, row)
    at_next = (section + 1, row)
    at_mirror = (mirror, row)

    inner = pl.ds(width, size)

    def load(src, dst, k):
        return pltpu.make_async_copy(src, dst, in_sem.at[k])

    load_act = load(act_hbm, act, 0)
    load_held = load(held_hbm, held, 1)
    load_grad = load(grad_hbm, grad, 2)
    load_saved = load(saved_hbm, field.at[KEPT, inner], 3)
    load_target = load(target_hbm, target, 4)

    load_w1 = load(w1_hbm, w1, 5)
    load_w2 = load(w2_hbm, w2, 6)
    for copy in (load_act, load_held, load_saved, load_w1, load_grad, load_target, load_w2):
        copy.start()

    barrier = pltpu.get_barrier_semaphore()
    partners = ((has_up, at_up), (has_down, at_down), (has_prev, at_prev), (has_next, at_next))
    count = jnp.int32(1)
    for cond, where in partners:
        @pl.when(cond)
        def _(where=where):
            pl.semaphore_signal(barrier, inc=1, device_id=where, device_id_type=MESH)
        count = count + cond.astype(jnp.int32)
    pl.semaphore_signal(barrier, inc=1, device_id=at_mirror, device_id_type=MESH)

    for k in range(5):
        @pl.when(jnp.logical_not(has_up))
        def _(k=k):
            field[k, pl.ds(0, width)] = jnp.zeros((width, channels), field.dtype)

        @pl.when(jnp.logical_not(has_down))
        def _(k=k):
            field[k, pl.ds(width + size, width)] = jnp.zeros((width, channels), field.dtype)

    def columns(n):
        return pl.ds(pl.multiple_of(n * part, part), part)

    def halo_up(k, n):
        return pltpu.make_async_remote_copy(
            src_ref=field.at[k, pl.ds(width, width), columns(n)],
            dst_ref=field.at[k, pl.ds(width + size, width), columns(n)],
            send_sem=halo_send.at[k, 0, n],
            recv_sem=halo_recv.at[k, 0, n],
            device_id=at_up,
            device_id_type=MESH,
        )

    def halo_down(k, n):
        return pltpu.make_async_remote_copy(
            src_ref=field.at[k, pl.ds(size, width), columns(n)],
            dst_ref=field.at[k, pl.ds(0, width), columns(n)],
            send_sem=halo_send.at[k, 1, n],
            recv_sem=halo_recv.at[k, 1, n],
            device_id=at_down,
            device_id_type=MESH,
        )

    def send_halo(k, n):
        @pl.when(has_up)
        def _():
            halo_up(k, n).start()

        @pl.when(has_down)
        def _():
            halo_down(k, n).start()

    def wait_halo(k):
        @pl.when(has_up)
        def _():
            for n in range(HALVES):
                halo_up(k, n).wait_send()
                halo_down(k, n).wait_recv()

        @pl.when(has_down)
        def _():
            for n in range(HALVES):
                halo_down(k, n).wait_send()
                halo_up(k, n).wait_recv()

    load_act.wait()
    load_held.wait()
    field[U, inner] = (act[...].astype(jnp.float32) + dec * held[...].astype(jnp.float32)).astype(field.dtype)
    pl.semaphore_wait(barrier, count)
    for n in range(HALVES):
        send_halo(U, n)
    load_saved.wait()
    load_grad.wait()

    @pl.when(not_last)
    def _():
        for n in range(HALVES):
            send_halo(KEPT, n)
        top = grad[...].astype(jnp.float32) + (1.0 - dec) * held[...].astype(jnp.float32)
        field[GTOP, inner] = top.astype(field.dtype)
        for n in range(HALVES):
            send_halo(GTOP, n)

    out_refs = (fwd_out, grad_out, mirror_out)

    tile = size // HALVES

    def place(c, offset=0):
        n, m = c // HALVES, c % HALVES
        return (pl.ds(pl.multiple_of(offset + m * tile, width), tile), columns(n))

    def deliver(src, kind, c, where):
        at = place(c)
        return pltpu.make_async_remote_copy(
            src_ref=src.at[at],
            dst_ref=out_refs[kind].at[at],
            send_sem=out_send.at[kind, c],
            recv_sem=out_recv.at[kind, c],
            device_id=where,
            device_id_type=MESH,
        )

    def product(k, w, flip, b, c):
        n, m = c // HALVES, c % HALVES
        x = [field[k, pl.ds(pl.multiple_of(m * tile + a * width, width), tile)] for a in range(3)]
        if flip:
            tap = [w[3 * (2 - a) + 2 - b, columns(n), :] for a in range(3)]
            dims = (((1,), (1,)), ((), ()))
        else:
            tap = [w[3 * a + b, :, columns(n)] for a in range(3)]
            dims = (((1,), (0,)), ((), ()))
        x, tap = jnp.concatenate(x, 1), jnp.concatenate(tap, 1 if flip else 0)
        return lax.dot_general(x, tap, dims, preferred_element_type=jnp.float32)

    def conv(k, w, flip, c):
        column = lax.broadcasted_iota(jnp.int32, (tile, 1), 0) % width
        left, centre, right = [product(k, w, flip, b, c) for b in range(3)]
        left = jnp.where(column == 0, 0.0, pltpu.roll(left, 1, 0))
        right = jnp.where(column == width - 1, 0.0, pltpu.roll(right, tile - 1, 0))
        return left + centre + right

    def run(k, body):
        wait_halo(k)

        def step(c, _):
            body(c)
            return 0

        lax.fori_loop(0, HALVES * HALVES, step, 0)

    def send_part(k, c):
        n, m = c // HALVES, c % HALVES

        @pl.when(jnp.logical_and(has_up, m == 0))
        def _():
            halo_up(k, n).start()

        @pl.when(jnp.logical_and(has_down, m == HALVES - 1))
        def _():
            halo_down(k, n).start()

    def step_hidden():
        def body(c):
            value = conv(U, w1, False, c)
            sig = jax.nn.sigmoid(value)
            at = place(c, width)
            field[HID, at[0], at[1]] = (value * sig).astype(field.dtype)
            slope[place(c)] = sig * (1.0 + value * (1.0 - sig))
            send_part(HID, c)

        run(U, body)

    def step_pre():
        def body(c):
            value = conv(KEPT, w1, False, c)
            sig = jax.nn.sigmoid(value)
            slope[place(c)] = sig * (1.0 + value * (1.0 - sig))

        run(KEPT, body)

    def step_output():
        def body(c):
            at = place(c)
            base = act[at].astype(jnp.float32) + dec * held[at].astype(jnp.float32)
            value = (base + conv(HID, w2, False, c)).astype(y.dtype)
            y[at] = value

            @pl.when(is_last)
            def _():
                top = value.astype(jnp.float32) - target[at].astype(jnp.float32)
                low_at = place(c, width)
                field[GTOP, low_at[0], low_at[1]] = top.astype(field.dtype)
                send_part(GTOP, c)

            @pl.when(jnp.logical_and(encoder, jnp.logical_not(middle)))
            def _():
                deliver(y, MIRROR, c, at_mirror).start()

            @pl.when(has_next)
            def _():
                deliver(y, FWD, c, at_next).start()

        run(HID, body)

    def step_back():
        def body(c):
            at = place(c, width)
            field[GMID, at[0], at[1]] = (slope[place(c)] * conv(GTOP, w2, True, c)).astype(field.dtype)
            send_part(GMID, c)

        run(GTOP, body)

    def step_low():
        def body(c):
            at = place(c, width)
            base = field[GTOP, at[0], at[1]].astype(jnp.float32)
            low[place(c)] = (base + conv(GMID, w1, True, c)).astype(low.dtype)

            @pl.when(jnp.logical_and(decoder, jnp.logical_not(middle)))
            def _():
                deliver(low, MIRROR, c, at_mirror).start()

            @pl.when(has_prev)
            def _():
                deliver(low, GRAD, c, at_prev).start()

        run(GMID, body)

    load_w1.wait()
    pl.when(others)(step_hidden)
    pl.when(not_last)(step_pre)
    load_target.wait()
    load_w2.wait()
    pl.when(others)(step_output)
    step_back()
    pl.when(inner_dec)(step_hidden)
    step_low()
    pl.when(inner_dec)(step_output)

    def drain(cond, src, kind, where, sent):
        @pl.when(cond)
        def _():
            for c in range(HALVES * HALVES):
                copy = deliver(src, kind, c, where)
                (copy.wait_send if sent else copy.wait_recv)()

    apart = jnp.logical_not(middle)
    drain(has_prev, y, FWD, at_next, False)
    drain(has_next, low, GRAD, at_prev, False)
    drain(apart, y, MIRROR, at_mirror, False)
    drain(has_next, y, FWD, at_next, True)
    drain(has_prev, low, GRAD, at_prev, True)
    drain(apart, y, MIRROR, at_mirror, True)


def finish_kernel(sections, pieces, fwd, grad, mirror, fwd_out, grad_out, mirror_out, zeros, sem):
    section = lax.axis_index("section")
    size = zeros.shape[0]
    piece = size // pieces
    is_first, is_last = section == 0, section == sections - 1
    middle_enc = section == sections // 2 - 1
    middle_dec = section == sections // 2
    apart = jnp.logical_not(jnp.logical_or(middle_enc, middle_dec))
    moves = (
        (jnp.logical_not(is_first), fwd, fwd_out, 0),
        (is_first, zeros, fwd_out, 0),
        (jnp.logical_not(is_last), grad, grad_out, 1),
        (is_last, zeros, grad_out, 1),
        (middle_dec, fwd, mirror_out, 2),
        (middle_enc, grad, mirror_out, 2),
        (apart, mirror, mirror_out, 2),
    )

    def copies(src, dst, k):
        for p in range(pieces):
            rows = pl.ds(p * piece, piece)
            yield pltpu.make_async_copy(src.at[rows], dst.at[rows], sem.at[k, p])

    @pl.when(jnp.logical_or(is_first, is_last))
    def _():
        zeros[...] = jnp.zeros_like(zeros)

    for cond, src, dst, k in moves:
        @pl.when(cond)
        def _(src=src, dst=dst, k=k):
            for copy in copies(src, dst, k):
                copy.start()
    for dst, k in ((fwd_out, 0), (grad_out, 1), (mirror_out, 2)):
        for copy in copies(zeros, dst, k):
            copy.wait()


def on_device(fwd_in, grad_in, saved_in, mirror_held, target, w_first, w_second):
    _, rows, width, channels = fwd_in.shape
    size = rows * width
    taps = w_first.shape[1] * w_first.shape[2]
    dtype = fwd_in.dtype
    sections = lax.axis_size("section")
    row_devices = lax.axis_size("rows")
    flat = lambda value: value.reshape(size, channels)
    flat_w = lambda value: value.reshape(taps, channels, channels)
    any_spec = pl.BlockSpec(memory_space=pl.ANY)
    hbm_spec = pl.BlockSpec(memory_space=pltpu.HBM)
    plane = pltpu.VMEM((size, channels), dtype)
    weight = pltpu.VMEM((taps, channels, channels), dtype)
    outs = pl.pallas_call(
        functools.partial(relay_kernel, sections, row_devices, width),
        out_shape=[jax.ShapeDtypeStruct((size, channels), dtype)] * 3,
        in_specs=[hbm_spec] * 7,
        out_specs=[any_spec] * 3,
        scratch_shapes=[
            plane, plane, plane, plane,
            weight, weight,
            pltpu.VMEM((5, size + 2 * width, channels), dtype),
            pltpu.VMEM((size, channels), jnp.float32),
            plane, plane,
            pltpu.SemaphoreType.DMA((7,)),
            pltpu.SemaphoreType.DMA((5, 2, HALVES)),
            pltpu.SemaphoreType.DMA((5, 2, HALVES)),
            pltpu.SemaphoreType.DMA((3, HALVES * HALVES)),
            pltpu.SemaphoreType.DMA((3, HALVES * HALVES)),
        ],
        compiler_params=pltpu.CompilerParams(
            collective_id=0, has_side_effects=True, vmem_limit_bytes=62 * 2**20
        ),
        cost_estimate=pl.CostEstimate(
            flops=10 * size * taps * channels * channels,
            bytes_accessed=4 * taps * channels * channels + 16 * size * channels,
            transcendentals=2 * size * channels,
        ),
    )(
        flat(fwd_in), flat(grad_in), flat(saved_in), flat(mirror_held), flat(target),
        flat_w(w_first), flat_w(w_second),
    )
    pieces = 2
    outs = pl.pallas_call(
        functools.partial(finish_kernel, sections, pieces),
        out_shape=[jax.ShapeDtypeStruct((size, channels), dtype)] * 3,
        in_specs=[pl.BlockSpec(memory_space=pltpu.VMEM)] * 3,
        out_specs=[hbm_spec] * 3,
        scratch_shapes=[plane, pltpu.SemaphoreType.DMA((3, pieces))],
        compiler_params=pltpu.CompilerParams(vmem_limit_bytes=62 * 2**20),
    )(*outs)
    return tuple(value.reshape(fwd_in.shape) for value in outs)


def solution(mesh):
    blocks = P("section", "rows", None, None)
    weights = P("section", None, None, None, None)
    return jax.shard_map(
        on_device,
        mesh=mesh,
        in_specs=(blocks, blocks, blocks, blocks, P("rows", None, None), weights, weights),
        out_specs=(blocks, blocks, blocks),
        check_vma=False,
    )
```

```python
import functools

import jax
import jax.numpy as jnp
from jax import lax
from jax.experimental import pallas as pl
from jax.experimental.pallas import tpu as pltpu
from jax.sharding import PartitionSpec as P

MESH = pl.DeviceIdType.MESH
U, KEPT, GTOP, HID, GMID = range(5)
FWD, GRAD, MIRROR = range(3)
HALVES = 2


def relay_kernel(
    sections, row_devices, width,
    act_hbm, grad_hbm, saved_hbm, held_hbm, target_hbm, w1_hbm, w2_hbm,
    fwd_out, grad_out, mirror_out,
    act, grad, held, target, w1, w2, field, slope, y, low,
    in_sem, halo_send, halo_recv, out_send, out_recv,
):
    size, channels = act.shape
    part = channels // HALVES
    section = lax.axis_index("section")
    row = lax.axis_index("rows")
    half_sections = sections // 2
    decoder = section >= half_sections
    is_last = section == sections - 1
    dec = decoder.astype(jnp.float32)
    has_up, has_down = row > 0, row < row_devices - 1
    has_prev, has_next = section > 0, section < sections - 1
    mirror = sections - 1 - section
    middle_enc = section == half_sections - 1
    middle_dec = section == half_sections
    middle = jnp.logical_or(middle_enc, middle_dec)
    encoder = jnp.logical_not(decoder)
    inner_dec = jnp.logical_and(decoder, jnp.logical_not(is_last))
    others = jnp.logical_not(inner_dec)
    not_last = jnp.logical_not(is_last)
    at_up = (section, row - 1)
    at_down = (section, row + 1)
    at_prev = (section - 1, row)
    at_next = (section + 1, row)
    at_mirror = (mirror, row)

    inner = pl.ds(width, size)

    def load(src, dst, k):
        return pltpu.make_async_copy(src, dst, in_sem.at[k])

    load_act = load(act_hbm, act, 0)
    load_held = load(held_hbm, held, 1)
    load_grad = load(grad_hbm, grad, 2)
    load_saved = load(saved_hbm, field.at[KEPT, inner], 3)
    load_target = load(target_hbm, target, 4)


    def load_half(j, n):
        src, dst = ((w1_hbm, w1), (w2_hbm, w2))[j]
        cut = pl.ds(n * part, part)
        return pltpu.make_async_copy(src.at[:, :, cut], dst.at[:, :, cut], in_sem.at[5 + HALVES * j + n])

    for copy in (load_act, load_held, load_half(0, 0), load_saved, load_half(0, 1), load_grad, load_target,
                 load_half(1, 0), load_half(1, 1)):
        copy.start()

    barrier = pltpu.get_barrier_semaphore()
    partners = ((has_up, at_up), (has_down, at_down), (has_prev, at_prev), (has_next, at_next))
    count = jnp.int32(1)
    for cond, where in partners:
        @pl.when(cond)
        def _(where=where):
            pl.semaphore_signal(barrier, inc=1, device_id=where, device_id_type=MESH)
        count = count + cond.astype(jnp.int32)
    pl.semaphore_signal(barrier, inc=1, device_id=at_mirror, device_id_type=MESH)

    for k in range(5):
        @pl.when(jnp.logical_not(has_up))
        def _(k=k):
            field[k, pl.ds(0, width)] = jnp.zeros((width, channels), field.dtype)

        @pl.when(jnp.logical_not(has_down))
        def _(k=k):
            field[k, pl.ds(width + size, width)] = jnp.zeros((width, channels), field.dtype)

    def columns(n):
        return pl.ds(pl.multiple_of(n * part, part), part)

    def halo_up(k, n):
        return pltpu.make_async_remote_copy(
            src_ref=field.at[k, pl.ds(width, width), columns(n)],
            dst_ref=field.at[k, pl.ds(width + size, width), columns(n)],
            send_sem=halo_send.at[k, 0, n],
            recv_sem=halo_recv.at[k, 0, n],
            device_id=at_up,
            device_id_type=MESH,
        )

    def halo_down(k, n):
        return pltpu.make_async_remote_copy(
            src_ref=field.at[k, pl.ds(size, width), columns(n)],
            dst_ref=field.at[k, pl.ds(0, width), columns(n)],
            send_sem=halo_send.at[k, 1, n],
            recv_sem=halo_recv.at[k, 1, n],
            device_id=at_down,
            device_id_type=MESH,
        )

    def send_halo(k, n):
        @pl.when(has_up)
        def _():
            halo_up(k, n).start()

        @pl.when(has_down)
        def _():
            halo_down(k, n).start()

    def wait_top(k):
        @pl.when(has_up)
        def _():
            for n in range(HALVES):
                halo_up(k, n).wait_send()
                halo_down(k, n).wait_recv()

    def wait_bottom(k):
        @pl.when(has_down)
        def _():
            for n in range(HALVES):
                halo_down(k, n).wait_send()
                halo_up(k, n).wait_recv()

    load_act.wait()
    load_held.wait()
    field[U, inner] = (act[...].astype(jnp.float32) + dec * held[...].astype(jnp.float32)).astype(field.dtype)
    pl.semaphore_wait(barrier, count)
    for n in range(HALVES):
        send_halo(U, n)
    load_saved.wait()
    load_grad.wait()

    @pl.when(not_last)
    def _():
        for n in range(HALVES):
            send_halo(KEPT, n)
        top = grad[...].astype(jnp.float32) + (1.0 - dec) * held[...].astype(jnp.float32)
        field[GTOP, inner] = top.astype(field.dtype)
        for n in range(HALVES):
            send_halo(GTOP, n)

    out_refs = (fwd_out, grad_out, mirror_out)

    tile = size // HALVES

    def place(c, offset=0):
        n, m = c // HALVES, c % HALVES
        return (pl.ds(pl.multiple_of(offset + m * tile, width), tile), columns(n))

    def deliver(src, kind, c, where):
        at = place(c)
        return pltpu.make_async_remote_copy(
            src_ref=src.at[at],
            dst_ref=out_refs[kind].at[at],
            send_sem=out_send.at[kind, c],
            recv_sem=out_recv.at[kind, c],
            device_id=where,
            device_id_type=MESH,
        )

    def product(k, w, flip, b, c):
        n, m = c // HALVES, c % HALVES
        x = [field[k, pl.ds(pl.multiple_of(m * tile + a * width, width), tile)] for a in range(3)]
        if flip:
            tap = [w[3 * (2 - a) + 2 - b, columns(n), :] for a in range(3)]
            dims = (((1,), (1,)), ((), ()))
        else:
            tap = [w[3 * a + b, :, columns(n)] for a in range(3)]
            dims = (((1,), (0,)), ((), ()))
        x, tap = jnp.concatenate(x, 1), jnp.concatenate(tap, 1 if flip else 0)
        return lax.dot_general(x, tap, dims, preferred_element_type=jnp.float32)

    def conv(k, w, flip, c):
        column = lax.broadcasted_iota(jnp.int32, (tile, 1), 0) % width
        left, centre, right = [product(k, w, flip, b, c) for b in range(3)]
        left = jnp.where(column == 0, 0.0, pltpu.roll(left, 1, 0))
        right = jnp.where(column == width - 1, 0.0, pltpu.roll(right, tile - 1, 0))
        return left + centre + right

    def run(k, body, turned, arrive=None):
        def step(i, _):
            n, m = i // HALVES, i % HALVES
            if turned:
                m = HALVES - 1 - m
            if arrive is not None:
                for h in range(HALVES):
                    @pl.when(jnp.logical_and(arrive, i == HALVES * h))
                    def _(h=h):
                        load_half(0, h).wait()

            @pl.when(i == int(turned))
            def _():
                wait_top(k)

            @pl.when(i == int(not turned))
            def _():
                wait_bottom(k)

            body(n * HALVES + m)
            return 0

        lax.fori_loop(0, HALVES * HALVES, step, 0)

    def sigmoid(value):
        return 0.5 + 0.5 * jnp.tanh(0.5 * value)

    def send_part(k, c):
        n, m = c // HALVES, c % HALVES

        @pl.when(jnp.logical_and(has_up, m == 0))
        def _():
            halo_up(k, n).start()

        @pl.when(jnp.logical_and(has_down, m == HALVES - 1))
        def _():
            halo_down(k, n).start()

    def step_hidden(arrive=None):
        def body(c):
            value = conv(U, w1, False, c)
            sig = sigmoid(value)
            at = place(c, width)
            field[HID, at[0], at[1]] = (value * sig).astype(field.dtype)
            slope[place(c)] = sig * (1.0 + value * (1.0 - sig))
            send_part(HID, c)

        run(U, body, False, arrive)

    def step_pre():
        def body(c):
            value = conv(KEPT, w1, False, c)
            sig = sigmoid(value)
            slope[place(c)] = sig * (1.0 + value * (1.0 - sig))

        run(KEPT, body, False, inner_dec)

    def step_output():
        def body(c):
            at = place(c)
            base = act[at].astype(jnp.float32) + dec * held[at].astype(jnp.float32)
            value = (base + conv(HID, w2, False, c)).astype(y.dtype)
            y[at] = value

            @pl.when(is_last)
            def _():
                top = value.astype(jnp.float32) - target[at].astype(jnp.float32)
                low_at = place(c, width)
                field[GTOP, low_at[0], low_at[1]] = top.astype(field.dtype)
                send_part(GTOP, c)

            @pl.when(jnp.logical_and(encoder, jnp.logical_not(middle)))
            def _():
                deliver(y, MIRROR, c, at_mirror).start()

            @pl.when(has_next)
            def _():
                deliver(y, FWD, c, at_next).start()

        run(HID, body, True)

    def step_back():
        def body(c):
            at = place(c, width)
            field[GMID, at[0], at[1]] = (slope[place(c)] * conv(GTOP, w2, True, c)).astype(field.dtype)
            send_part(GMID, c)

        run(GTOP, body, False)

    def step_low():
        def body(c):
            at = place(c, width)
            base = field[GTOP, at[0], at[1]].astype(jnp.float32)
            low[place(c)] = (base + conv(GMID, w1, True, c)).astype(low.dtype)

            @pl.when(jnp.logical_and(decoder, jnp.logical_not(middle)))
            def _():
                deliver(low, MIRROR, c, at_mirror).start()

            @pl.when(has_prev)
            def _():
                deliver(low, GRAD, c, at_prev).start()

        run(GMID, body, True)

    pl.when(others)(lambda: step_hidden(others))
    pl.when(not_last)(step_pre)
    load_target.wait()
    for h in range(HALVES):
        load_half(1, h).wait()
    pl.when(others)(step_output)
    step_back()
    pl.when(inner_dec)(step_hidden)
    step_low()
    pl.when(inner_dec)(step_output)

    def drain(cond, src, kind, where, sent):
        @pl.when(cond)
        def _():
            for c in range(HALVES * HALVES):
                copy = deliver(src, kind, c, where)
                (copy.wait_send if sent else copy.wait_recv)()

    apart = jnp.logical_not(middle)
    drain(has_prev, y, FWD, at_next, False)
    drain(has_next, low, GRAD, at_prev, False)
    drain(apart, y, MIRROR, at_mirror, False)
    drain(has_next, y, FWD, at_next, True)
    drain(has_prev, low, GRAD, at_prev, True)
    drain(apart, y, MIRROR, at_mirror, True)


def finish_kernel(sections, pieces, fwd, grad, mirror, fwd_out, grad_out, mirror_out, stage, in_sem, sem):
    section = lax.axis_index("section")
    size = stage.shape[1]
    piece = size // pieces
    is_first, is_last = section == 0, section == sections - 1
    middle_enc = section == sections // 2 - 1
    middle_dec = section == sections // 2
    has_prev, has_next = jnp.logical_not(is_first), jnp.logical_not(is_last)
    apart = jnp.logical_not(jnp.logical_or(middle_enc, middle_dec))
    sources = ((has_prev, fwd, 0), (has_next, grad, 1), (apart, mirror, 2))

    def fetch(src, k, p):
        rows = pl.ds(p * piece, piece)
        return pltpu.make_async_copy(src.at[rows], stage.at[k, rows], in_sem.at[k, p])

    def put(k, dst, where, p):
        rows = pl.ds(p * piece, piece)
        return pltpu.make_async_copy(stage.at[k, rows], dst.at[rows], sem.at[where, p])

    for p in range(pieces):
        for cond, src, k in sources:
            @pl.when(cond)
            def _(src=src, k=k, p=p):
                fetch(src, k, p).start()

    @pl.when(is_first)
    def _():
        stage[0] = jnp.zeros(stage.shape[1:], stage.dtype)

    @pl.when(is_last)
    def _():
        stage[1] = jnp.zeros(stage.shape[1:], stage.dtype)

    for p in range(pieces):
        for cond, src, k in sources:
            @pl.when(cond)
            def _(src=src, k=k, p=p):
                fetch(src, k, p).wait()
        put(0, fwd_out, 0, p).start()
        put(1, grad_out, 1, p).start()
        for cond, k in ((middle_dec, 0), (middle_enc, 1), (apart, 2)):
            @pl.when(cond)
            def _(k=k, p=p):
                put(k, mirror_out, 2, p).start()
    for p in range(pieces):
        put(0, fwd_out, 0, p).wait()
        put(1, grad_out, 1, p).wait()
        put(2, mirror_out, 2, p).wait()


def on_device(fwd_in, grad_in, saved_in, mirror_held, target, w_first, w_second):
    _, rows, width, channels = fwd_in.shape
    size = rows * width
    taps = w_first.shape[1] * w_first.shape[2]
    dtype = fwd_in.dtype
    sections = lax.axis_size("section")
    row_devices = lax.axis_size("rows")
    flat = lambda value: value.reshape(size, channels)
    flat_w = lambda value: value.reshape(taps, channels, channels)
    any_spec = pl.BlockSpec(memory_space=pl.ANY)
    hbm_spec = pl.BlockSpec(memory_space=pltpu.HBM)
    plane = pltpu.VMEM((size, channels), dtype)
    weight = pltpu.VMEM((taps, channels, channels), dtype)
    outs = pl.pallas_call(
        functools.partial(relay_kernel, sections, row_devices, width),
        out_shape=[jax.ShapeDtypeStruct((size, channels), dtype)] * 3,
        in_specs=[hbm_spec] * 7,
        out_specs=[any_spec] * 3,
        scratch_shapes=[
            plane, plane, plane, plane,
            weight, weight,
            pltpu.VMEM((5, size + 2 * width, channels), dtype),
            pltpu.VMEM((size, channels), jnp.float32),
            plane, plane,
            pltpu.SemaphoreType.DMA((5 + 2 * HALVES,)),
            pltpu.SemaphoreType.DMA((5, 2, HALVES)),
            pltpu.SemaphoreType.DMA((5, 2, HALVES)),
            pltpu.SemaphoreType.DMA((3, HALVES * HALVES)),
            pltpu.SemaphoreType.DMA((3, HALVES * HALVES)),
        ],
        compiler_params=pltpu.CompilerParams(
            collective_id=0, has_side_effects=True, vmem_limit_bytes=62 * 2**20
        ),
        cost_estimate=pl.CostEstimate(
            flops=10 * size * taps * channels * channels,
            bytes_accessed=4 * taps * channels * channels + 16 * size * channels,
            transcendentals=2 * size * channels,
        ),
    )(
        flat(fwd_in), flat(grad_in), flat(saved_in), flat(mirror_held), flat(target),
        flat_w(w_first), flat_w(w_second),
    )
    pieces = 4
    outs = pl.pallas_call(
        functools.partial(finish_kernel, sections, pieces),
        out_shape=[jax.ShapeDtypeStruct((size, channels), dtype)] * 3,
        in_specs=[any_spec] * 3,
        out_specs=[hbm_spec] * 3,
        scratch_shapes=[
            pltpu.VMEM((3, size, channels), dtype),
            pltpu.SemaphoreType.DMA((3, pieces)),
            pltpu.SemaphoreType.DMA((3, pieces)),
        ],
        compiler_params=pltpu.CompilerParams(vmem_limit_bytes=62 * 2**20),
    )(*outs)
    return tuple(value.reshape(fwd_in.shape) for value in outs)


def solution(mesh):
    blocks = P("section", "rows", None, None)
    weights = P("section", None, None, None, None)
    return jax.shard_map(
        on_device,
        mesh=mesh,
        in_specs=(blocks, blocks, blocks, blocks, P("rows", None, None), weights, weights),
        out_specs=(blocks, blocks, blocks),
        check_vma=False,
    )
```
